32 devices in a mesh: pipe: 8 (over z, x), ctx: 4 (over y, core).
Axes of the slice: x: 2, y: 2, z: 4, core: 2. Of those that a mesh axis runs over, the one named last changes fastest.
Arguments:
- forward_in: bfloat16 [8, 2, 512, 8192], P('pipe', None, 'ctx'), may hold values from -8 to 8
- backward_in: bfloat16 [8, 2, 512, 8192], P('pipe', None, 'ctx'), may hold values from -8 to 8
- grad_out: bfloat16 [8, 2, 512, 8192], P('pipe', None, 'ctx'), may hold values from -6 to 6
- cached_keys: bfloat16 [8, 2, 512, 8, 128], P('pipe', None, 'ctx'), may hold values from -21 to 21
- cached_values: bfloat16 [8, 2, 512, 8, 128], P('pipe', None, 'ctx'), may hold values from -6 to 6
- norm_gain: float32 [8, 2, 8192], P('pipe'), may hold values from 0.25 to 1.75
- key_weight: bfloat16 [8, 2, 8192, 1024], P('pipe', None, 'ctx'), may hold values from -0.0625 to 0.0625
- value_weight: bfloat16 [8, 2, 8192, 1024], P('pipe', None, 'ctx'), may hold values from -0.0625 to 0.0625
- segment_index: int32 [8, 2, 2], P('pipe'), may hold values from 0 to 1, as said below
Outputs:
- next_forward: bfloat16 [8, 2, 512, 8192], P('pipe', None, 'ctx')
- next_backward: bfloat16 [8, 2, 512, 8192], P('pipe', None, 'ctx')
The draws below stay inside these ranges and needn't reach their ends.
Inputs may be any that keep to these rules, and one draw needn't show every extreme that they name: `segment_index`: the largest segment index, 1, occurs in every draw.
All inputs are finite; a program needn't handle non-finite values.
Results may differ from the reference program's by a relative error of at most 0.04.
Values may be sent and summed in bfloat16 or wider, within the bound.
A program may use at most 256 MiB of HBM per device.

```python
import jax
import jax.numpy as jnp
from jax import lax

D = 8192
H = 64
KVH = 8
HS = 128
SEG = 512
STRETCHES = 2
CACHE = 512
N_PIPE = 8
N_CTX = 4


def residual_rows(key, shape):
    first_key = jax.random.fold_in(key, 101)
    values = jnp.clip(jax.random.normal(first_key, shape, jnp.float32), -6.0, 6.0)
    return values.astype(jnp.bfloat16)


def draw_forward_in(key, part):
    return residual_rows(jax.random.fold_in(key, 1), (N_PIPE, STRETCHES, SEG, D))


def draw_backward_in(key, part):
    return residual_rows(jax.random.fold_in(key, 2), (N_PIPE, STRETCHES, SEG, D))


def draw_cached_keys(key, part):
    shape = (N_PIPE, STRETCHES, CACHE, KVH, HS)
    first_key = jax.random.fold_in(key, 201)
    values = jnp.clip(jax.random.normal(first_key, shape, jnp.float32), -6.0, 6.0)
    return values.astype(jnp.bfloat16)


def draw_segment_index(key, part):
    highest = CACHE // SEG
    count = N_PIPE * STRETCHES * 2
    drawn = jax.random.randint(jax.random.fold_in(key, 301), (count,), 0, highest + 1)
    spot = jax.random.randint(jax.random.fold_in(key, 302), (), 0, count)
    places = jnp.arange(count, dtype=jnp.int32)
    drawn = jnp.where(places == spot, highest, drawn)
    return drawn.reshape(N_PIPE, STRETCHES, 2).astype(jnp.int32)


def level_of(rng, extent, cuts, smallest, high):
    def one(dim, shards_of):
        heights = jax.random.uniform(jax.random.fold_in(jax.random.fold_in(rng, 6), dim), (shards_of,), jnp.float32, smallest / len(cuts), high / len(cuts))
        return jnp.repeat(jnp.exp(heights), extent[dim] // shards_of).reshape((-1,) + (1,) * (len(extent) - dim - 1))

    gain = one(*cuts[0])
    for cut in cuts[1:]:
        gain = gain * one(*cut)
    return gain


def scatter_about(key, dims, deviation, bound, shards=(), kind=jnp.bfloat16):
    values = deviation * jax.random.normal(key, dims, jnp.float32)
    if shards:
        values = values * level_of(key, dims, shards, -0.22, 0.18)
    return jnp.clip(values, -bound, bound).astype(kind)


def setup_inputs(seed: int = 0) -> dict:
    seeds = jax.random.split(jax.random.key(seed), 10)
    return {
        "forward_in": draw_forward_in(jax.random.fold_in(seeds[9], 71), 0),
        "backward_in": draw_backward_in(jax.random.fold_in(seeds[9], 71), 0),
        "grad_out": scatter_about(seeds[2], (N_PIPE, STRETCHES, SEG, D), 1.0, 6.0, ((0, 8), (2, 4))),
        "cached_keys": draw_cached_keys(jax.random.fold_in(seeds[9], 71), 0),
        "cached_values": scatter_about(seeds[4], (N_PIPE, STRETCHES, CACHE, KVH, HS), 1.0, 6.0, ((0, 8), (2, 4))),
        "norm_gain": jnp.clip(1.0 + 0.15 * jax.random.normal(seeds[5], (N_PIPE, STRETCHES, D), jnp.float32), 0.25, 1.75),
        "key_weight": scatter_about(seeds[6], (N_PIPE, STRETCHES, D, KVH * HS), D ** -0.5, 0.0625, ((0, 8), (2, 4))),
        "value_weight": scatter_about(seeds[7], (N_PIPE, STRETCHES, D, KVH * HS), D ** -0.5, 0.0625, ((0, 8), (2, 4))),
        "segment_index": draw_segment_index(jax.random.fold_in(seeds[9], 71), 0),
    }


NEGATIVE = -1e+30

def normalize(in_rows, gain_row):
    as_float = in_rows.astype(jnp.float32)
    inverse = lax.rsqrt(lax.optimization_barrier(jnp.mean(as_float * as_float, axis=-1, keepdims=True)) + 1e-05)
    normed = as_float * inverse
    return (normed, inverse, (normed * gain_row).astype(jnp.bfloat16))

def block_product(activations, weight):
    tokens = activations.shape[0]
    pieces = activations.reshape(tokens, N_CTX, D // N_CTX).astype(jnp.float32)
    weight_pieces = weight.reshape(N_CTX, D // N_CTX, KVH * HS).astype(jnp.float32)
    partial_value = jnp.einsum('tnf,nfe->nte', pieces, weight_pieces)
    rounded = lax.optimization_barrier(partial_value.astype(jnp.bfloat16)).astype(jnp.float32)
    return lax.optimization_barrier(jnp.sum(rounded, axis=0)).astype(jnp.bfloat16)

def project_kv(activations, key_weight, value_weight):
    tokens = activations.shape[0]
    new_keys = block_product(activations, key_weight)
    new_values = block_product(activations, value_weight)
    return (new_keys.reshape(tokens, KVH, HS), new_values.reshape(tokens, KVH, HS))

def probabilities(queries, key_list, position):
    factor = HS ** (-0.5)
    scores = jnp.einsum('tkgd,skd->kgts', queries.astype(jnp.float32), key_list.astype(jnp.float32)) * factor
    column = lax.broadcasted_iota(jnp.int32, (SEG, key_list.shape[0]), 1)
    row_ids = lax.broadcasted_iota(jnp.int32, (SEG, key_list.shape[0]), 0)
    visible = jnp.where(column < CACHE, column < position * SEG, column - CACHE <= row_ids)
    scores = jnp.where(visible, scores, NEGATIVE)
    row_max = lax.optimization_barrier(jnp.max(scores, axis=-1, keepdims=True))
    lifted = jnp.exp(scores - row_max)
    return lifted / lax.optimization_barrier(jnp.sum(lifted, axis=-1, keepdims=True))

def attend(queries, key_list, value_list, position):
    prob_full = probabilities(queries, key_list, position)
    prob_half = prob_full.astype(jnp.bfloat16)
    attended = jnp.einsum('kgts,skd->tkgd', prob_half.astype(jnp.float32), value_list.astype(jnp.float32))
    return (prob_full, prob_half, attended.astype(jnp.bfloat16))

def run_total(per_head):
    run_len = min(H // N_CTX, H // KVH)
    tokens = per_head.shape[0]
    runs = per_head.reshape(tokens, KVH, H // KVH // run_len, run_len, HS)
    partial_sums = lax.optimization_barrier(lax.optimization_barrier(jnp.sum(runs, axis=3)).astype(jnp.bfloat16)).astype(jnp.float32)
    return lax.optimization_barrier(jnp.sum(partial_sums, axis=2)).astype(jnp.bfloat16)

def attend_back(queries, key_list, value_list, position, grad_heads):
    prob_full, prob_half, attended = attend(queries, key_list, value_list, position)
    grad_wide = grad_heads.astype(jnp.float32)
    grad_prob = jnp.einsum('tkgd,skd->kgts', grad_wide, value_list.astype(jnp.float32))
    row_delta = lax.optimization_barrier(jnp.sum(grad_wide * attended.astype(jnp.float32), axis=-1))
    row_delta = jnp.transpose(row_delta, (1, 2, 0))[..., None]
    grad_score = (prob_full * (grad_prob - row_delta) * HS ** (-0.5)).astype(jnp.bfloat16)
    grad_query = jnp.einsum('kgts,skd->tkgd', grad_score.astype(jnp.float32), key_list.astype(jnp.float32)).astype(jnp.bfloat16)
    own_score = grad_score[..., CACHE:].astype(jnp.float32)
    own_weight = prob_half[..., CACHE:].astype(jnp.float32)
    key_heads = jnp.einsum('kgts,tkgd->skgd', own_score, queries.astype(jnp.float32))
    value_heads = jnp.einsum('kgts,tkgd->skgd', own_weight, grad_wide)
    return (grad_query, run_total(key_heads), run_total(value_heads))

def input_grad(in_rows, gain_row, key_weight, value_weight, grad_query, grad_key, grad_value, grad_rows):
    parts = normalize(in_rows, gain_row)
    normed = parts[0]
    inverse = parts[1]
    tokens = in_rows.shape[0]
    back_rows = jnp.dot(grad_key.reshape(tokens, KVH * HS), key_weight.T, preferred_element_type=jnp.float32)
    back_rows = back_rows + jnp.dot(grad_value.reshape(tokens, KVH * HS), value_weight.T, preferred_element_type=jnp.float32)
    grad_acts = (grad_query.astype(jnp.float32).reshape(tokens, D) + back_rows).astype(jnp.bfloat16)
    grad_normed = grad_acts.astype(jnp.float32) * gain_row
    grad_input = inverse * (grad_normed - normed * lax.optimization_barrier(jnp.mean(grad_normed * normed, axis=-1, keepdims=True)))
    return (grad_rows.astype(jnp.float32) + grad_input).astype(jnp.bfloat16)

def one_section(section_args):
    forward_rows, backward_rows, grad_rows, keys_cached, values_cached, gain_row, key_weight, value_weight, section_segments = section_args
    forward_acts = normalize(forward_rows, gain_row)[2]
    forward_keys, forward_values = project_kv(forward_acts, key_weight, value_weight)
    key_list = jnp.concatenate([keys_cached, forward_keys], axis=0)
    value_list = jnp.concatenate([values_cached, forward_values], axis=0)
    attended = attend(forward_acts.reshape(SEG, KVH, H // KVH, HS), key_list, value_list, section_segments[0])[2]
    section_out = (forward_rows.astype(jnp.float32) + attended.reshape(SEG, D).astype(jnp.float32)).astype(jnp.bfloat16)
    backward_acts = normalize(backward_rows, gain_row)[2]
    backward_keys, backward_values = project_kv(backward_acts, key_weight, value_weight)
    back_keys = jnp.concatenate([keys_cached, backward_keys], axis=0)
    back_values = jnp.concatenate([values_cached, backward_values], axis=0)
    grad_query, grad_key, grad_value = attend_back(backward_acts.reshape(SEG, KVH, H // KVH, HS), back_keys, back_values, section_segments[1], grad_rows.reshape(SEG, KVH, H // KVH, HS))
    section_grad = input_grad(backward_rows, gain_row, key_weight, value_weight, grad_query, grad_key, grad_value, grad_rows)
    return (section_out, section_grad)

def flatten(block):
    swapped = jnp.swapaxes(block, 0, 1)
    return swapped.reshape((STRETCHES * N_PIPE,) + block.shape[2:])

def unflatten(stacked):
    return jnp.swapaxes(stacked.reshape((STRETCHES, N_PIPE) + stacked.shape[1:]), 0, 1)

def reference(forward_in, backward_in, grad_out, cached_keys, cached_values, norm_gain, key_weight, value_weight, segment_index):
    stacked = tuple((flatten(member) for member in (forward_in, backward_in, grad_out, cached_keys, cached_values, norm_gain, key_weight, value_weight, segment_index)))
    outs_forward, outs_backward = lax.map(one_section, stacked)
    next_forward = unflatten(jnp.roll(outs_forward, 1, axis=0))
    next_backward = unflatten(jnp.roll(outs_backward, -1, axis=0))
    return (next_forward, next_backward)
```

```python
import functools

import jax
import jax.numpy as jnp
from jax import lax
from jax.experimental import pallas as pl
from jax.experimental.pallas import tpu as pltpu
from jax.sharding import PartitionSpec as P

NEGATIVE = -1e30
LOG2_E = 1.4426950408889634
EPSILON = 1e-05
VMEM_LIMIT = 50 * 1024 * 1024


def call(kernel, grid, in_specs, out_specs, out_shape, scratch=(), flops=0, moved=0, name=None):
    return pl.pallas_call(
        kernel,
        grid=grid,
        in_specs=in_specs,
        out_specs=out_specs,
        out_shape=out_shape,
        scratch_shapes=list(scratch),
        compiler_params=pltpu.CompilerParams(
            vmem_limit_bytes=VMEM_LIMIT,
            dimension_semantics=("arbitrary",) * len(grid),
        ),
        cost_estimate=pl.CostEstimate(flops=int(flops), bytes_accessed=int(moved), transcendentals=0),
        name=name,
    )


def half(shape):
    return jax.ShapeDtypeStruct(shape, jnp.bfloat16)


def nt_dot(a, b):
    return lax.dot_general(a, b, (((1,), (1,)), ((), ())), preferred_element_type=jnp.float32)


def tn_dot(a, b):
    return lax.dot_general(a, b, (((0,), (0,)), ((), ())), preferred_element_type=jnp.float32)


def nn_dot(a, b):
    return jnp.dot(a, b, preferred_element_type=jnp.float32)


def norm_kernel(stretch, count, width, has_grad, *refs):
    rows_ref, gain_ref = refs[0], refs[1]
    acts_ref = refs[-2] if has_grad else refs[-1]
    rows = rows_ref[0, 0].astype(jnp.float32)
    inverse = lax.rsqrt(jnp.mean(rows * rows, axis=-1, keepdims=True) + EPSILON)
    acts = (rows * inverse * gain_ref[0, stretch : stretch + 1, :]).astype(jnp.bfloat16)
    for r in range(count):
        acts_ref[r] = acts[:, r * width : (r + 1) * width]
        if has_grad:
            refs[-1][r] = refs[2][0, 0, :, r * width : (r + 1) * width]


def norm_rows(rows, gain, stretch, count, grad=None):
    local_rows, model = rows.shape[2], rows.shape[3]
    width = model // count
    step = min(32, local_rows)
    row_spec = pl.BlockSpec((1, 1, step, model), lambda i: (0, stretch, i, 0))
    out_spec = pl.BlockSpec((count, step, width), lambda i: (0, i, 0))
    shape = half((count, local_rows, width))
    has_grad = grad is not None
    return call(
        functools.partial(norm_kernel, stretch, count, width, has_grad),
        (local_rows // step,),
        [row_spec, pl.BlockSpec(gain.shape, lambda i: (0, 0, 0))] + [row_spec] * has_grad,
        (out_spec, out_spec) if has_grad else out_spec,
        (shape, shape) if has_grad else shape,
        flops=6 * local_rows * model,
        moved=4 * local_rows * model * (1 + has_grad),
        name="norm_rows",
    )(*((rows, gain) + ((grad,) if has_grad else ())))


def project_kernel(kv_width, acts_ref, key_ref, value_ref, out_ref):
    acts = acts_ref[...]
    out_ref[0, :, :kv_width] = nn_dot(acts, key_ref[0, 0]).astype(jnp.bfloat16)
    out_ref[0, :, kv_width:] = nn_dot(acts, value_ref[0, 0]).astype(jnp.bfloat16)


def project(acts, key_weight, value_weight, stretch, count, kv_width, copies):
    tokens, width = acts.shape
    weight_spec = pl.BlockSpec((1, 1, width, kv_width), lambda r: (0, stretch, 0, r // copies))
    return call(
        functools.partial(project_kernel, kv_width),
        (count,),
        [pl.BlockSpec((tokens, width), lambda r: (0, 0)), weight_spec, weight_spec],
        pl.BlockSpec((1, tokens, 2 * kv_width), lambda r: (r, 0, 0)),
        half((count, tokens, 2 * kv_width)),
        flops=4 * tokens * width * kv_width * count,
        moved=2 * (tokens * width + 2 * width * kv_width * count + 2 * tokens * kv_width * count),
        name="project_kv",
    )(acts, key_weight, value_weight)


def load_lists(count, new_key, new_value, old_key, old_value, keys, values, own_keys, own_values):
    for new, old, kept, own in (
        (new_key, old_key, keys, own_keys),
        (new_value, old_value, values, own_values),
    ):
        total = new[0].astype(jnp.float32)
        for r in range(1, count):
            total = total + new[r].astype(jnp.float32)
        own[...] = total.astype(jnp.bfloat16)
        cached = old[:, 0, 0]
        kept[...] = cached.reshape(kept.shape)


def score_pieces(queries, start, rows, cached, keys, own_keys):
    pieces = []
    if cached:
        pieces.append(nt_dot(queries, keys[...]))
    if start:
        pieces.append(nt_dot(queries, own_keys[:start]))
    diagonal = nt_dot(queries, own_keys[start : start + rows])
    column = lax.broadcasted_iota(jnp.int32, (rows, rows), 1)
    row_ids = lax.broadcasted_iota(jnp.int32, (rows, rows), 0)
    pieces.append(jnp.where(column <= row_ids, diagonal, NEGATIVE))
    return pieces


def lifted_pieces(pieces, scale):
    row_max = pieces[0].max(axis=-1, keepdims=True)
    for piece in pieces[1:]:
        row_max = jnp.maximum(row_max, piece.max(axis=-1, keepdims=True))
    lifted = [jnp.exp2((piece - row_max) * scale) for piece in pieces]
    total = lifted[0].sum(axis=-1, keepdims=True)
    for piece in lifted[1:]:
        total = total + piece.sum(axis=-1, keepdims=True)
    return lifted, 1.0 / total


def list_pieces(start, rows, cached, kept, own):
    pieces = [kept[...]] if cached else []
    if start:
        pieces.append(own[:start])
    pieces.append(own[start : start + rows])
    return pieces


def sum_of(terms):
    total = terms[0]
    for term in terms[1:]:
        total = total + term
    return total


def attend_kernel(
    count, head, rows, per_step, place, segment, q_ref, nk, nv, ok, ov, out_ref, keys, values, own_keys, own_values
):
    @pl.when(pl.program_id(1) == 0)
    def _():
        load_lists(count, nk, nv, ok, ov, keys, values, own_keys, own_values)

    scale = head**-0.5 * LOG2_E
    tokens = q_ref.shape[0]

    def work(cached):
        for h in range(per_step):
            cols = slice(h * head, (h + 1) * head)
            for start in range(0, tokens, rows):
                part = slice(start, start + rows)
                queries = q_ref[part, cols]
                lifted, inverse = lifted_pieces(
                    score_pieces(queries, start, rows, cached, keys, own_keys), scale
                )
                value_pieces = list_pieces(start, rows, cached, values, own_values)
                attended = sum_of(
                    [nn_dot(e.astype(jnp.bfloat16), v) for e, v in zip(lifted, value_pieces)]
                )
                out_ref[part, cols] = (attended * inverse).astype(jnp.bfloat16)

    visible = segment[0, place[0], place[1]] > 0
    pl.when(visible)(lambda: work(True))
    pl.when(jnp.logical_not(visible))(lambda: work(False))


def attend_back_kernel(
    count, head, rows, per_step, place, segment, q_ref, g_ref, nk, nv, ok, ov,
    dq_ref, kv_ref, keys, values, own_keys, own_values, key_sum, value_sum
):
    @pl.when(pl.program_id(1) == 0)
    def _():
        load_lists(count, nk, nv, ok, ov, keys, values, own_keys, own_values)
        key_sum[...] = jnp.zeros_like(key_sum)
        value_sum[...] = jnp.zeros_like(value_sum)

    factor = head**-0.5
    tokens = q_ref.shape[0]

    def work(cached):
        for h in range(per_step):
            cols = slice(h * head, (h + 1) * head)
            for start in range(0, tokens, rows):
                part = slice(start, start + rows)
                queries = q_ref[part, cols]
                grads = g_ref[part, cols]
                lifted, inverse = lifted_pieces(
                    score_pieces(queries, start, rows, cached, keys, own_keys), factor * LOG2_E
                )
                value_pieces = list_pieces(start, rows, cached, values, own_values)
                key_pieces = list_pieces(start, rows, cached, keys, own_keys)
                rounded = [e.astype(jnp.bfloat16) for e in lifted]
                attended = sum_of([nn_dot(e, v) for e, v in zip(rounded, value_pieces)]) * inverse
                wide = grads.astype(jnp.float32)
                delta = jnp.sum(wide * attended, axis=-1, keepdims=True)
                scores = [
                    (e * (nt_dot(grads, v) - delta)).astype(jnp.bfloat16)
                    for e, v in zip(lifted, value_pieces)
                ]
                row_scale = inverse * factor
                dq = sum_of([nn_dot(s, k) for s, k in zip(scores, key_pieces)]) * row_scale
                dq_ref[part, cols] = dq.astype(jnp.bfloat16)
                scaled_q = (queries.astype(jnp.float32) * row_scale).astype(jnp.bfloat16)
                scaled_g = (wide * inverse).astype(jnp.bfloat16)
                if start:
                    key_sum[:start] += tn_dot(scores[-2], scaled_q)
                    value_sum[:start] += tn_dot(rounded[-2], scaled_g)
                key_sum[part] += tn_dot(scores[-1], scaled_q)
                value_sum[part] += tn_dot(rounded[-1], scaled_g)

    visible = segment[0, place[0], place[1]] > 0
    pl.when(visible)(lambda: work(True))
    pl.when(jnp.logical_not(visible))(lambda: work(False))

    @pl.when(pl.program_id(1) == pl.num_programs(1) - 1)
    def _():
        kv_ref[0] = key_sum[...].astype(jnp.bfloat16)
        kv_ref[1] = value_sum[...].astype(jnp.bfloat16)


def attention(segment, place, queries, new_kv, cache, kv_local, head, grads=None):
    tokens, width = queries.shape
    count, cache_local = cache.shape[0], cache.shape[3]
    cache_len = count * cache_local
    sub_heads = width // head // kv_local
    per_step = 2 if sub_heads % 2 == 0 else 1
    steps = sub_heads // per_step
    rows = min(256, tokens)
    stretch = place[0]
    head_spec = pl.BlockSpec((tokens, per_step * head), lambda j, g: (0, j * steps + g))
    in_specs = [pl.BlockSpec(memory_space=pltpu.SMEM), head_spec] + [head_spec] * (grads is not None)
    in_specs += [
        pl.BlockSpec((count, tokens, head), lambda j, g: (0, 0, j)),
        pl.BlockSpec((count, tokens, head), lambda j, g: (0, 0, kv_local + j)),
        pl.BlockSpec((count, 1, 1, cache_local, head), lambda j, g: (0, 0, stretch, 0, j)),
        pl.BlockSpec((count, 1, 1, cache_local, head), lambda j, g: (0, 1, stretch, 0, j)),
    ]
    scratch = [pltpu.VMEM((cache_len, head), jnp.bfloat16)] * 2
    scratch += [pltpu.VMEM((tokens, head), jnp.bfloat16)] * 2
    tail = (new_kv, new_kv, cache, cache)
    unit = 2 * tokens * width * (cache_len + tokens)
    if grads is None:
        return call(
            functools.partial(attend_kernel, count, head, rows, per_step, place),
            (kv_local, steps),
            in_specs,
            head_spec,
            half((tokens, width)),
            scratch,
            flops=2 * unit,
            moved=4 * tokens * width,
            name="attend",
        )(segment, queries, *tail)
    return call(
        functools.partial(attend_back_kernel, count, head, rows, per_step, place),
        (kv_local, steps),
        in_specs,
        (head_spec, pl.BlockSpec((2, tokens, head), lambda j, g: (0, 0, j))),
        (half((tokens, width)), half((2, tokens, kv_local * head))),
        scratch + [pltpu.VMEM((tokens, head), jnp.float32)] * 2,
        flops=5 * unit,
        moved=8 * tokens * width,
        name="attend_back",
    )(segment, queries, grads, *tail)


def back_kernel(count, copies, dq_ref, every_ref, key_ref, value_ref, out_ref, totals):
    kv_width = every_ref.shape[3]

    @pl.when(pl.program_id(0) == 0)
    def _():
        for which in range(2):
            for j in range(count // copies):
                total = every_ref[j * copies, which].astype(jnp.float32)
                for extra in range(1, copies):
                    total = total + every_ref[j * copies + extra, which].astype(jnp.float32)
                totals[which, :, j * kv_width : (j + 1) * kv_width] = total.astype(jnp.bfloat16)

    back = nt_dot(totals[0], key_ref[0, 0]) + nt_dot(totals[1], value_ref[0, 0])
    out_ref[...] = (dq_ref[...].astype(jnp.float32) + back).astype(jnp.bfloat16)


def back_rows(dq, every, key_weight, value_weight, stretch, copies):
    tokens, width = dq.shape
    count = every.shape[0]
    kv_total = key_weight.shape[3]
    step = min(512, width)
    weight_spec = pl.BlockSpec((1, 1, step, kv_total), lambda n: (0, stretch, n, 0))
    tile_spec = pl.BlockSpec((tokens, step), lambda n: (0, n))
    return call(
        functools.partial(back_kernel, count, copies),
        (width // step,),
        [tile_spec, pl.BlockSpec(every.shape, lambda n: (0, 0, 0, 0)), weight_spec, weight_spec],
        tile_spec,
        half((tokens, width)),
        [pltpu.VMEM((2, tokens, kv_total), jnp.bfloat16)],
        flops=4 * tokens * width * kv_total,
        moved=4 * tokens * width + 4 * width * kv_total,
        name="back_rows",
    )(dq, every, key_weight, value_weight)


def add_kernel(count, width, rows_ref, attn_ref, out_ref):
    for r in range(count):
        cols = slice(r * width, (r + 1) * width)
        out_ref[:, cols] = (
            rows_ref[0, 0, :, cols].astype(jnp.float32) + attn_ref[r].astype(jnp.float32)
        ).astype(jnp.bfloat16)


def add_rows(rows, attn, stretch):
    local_rows, model = rows.shape[2], rows.shape[3]
    count, width = attn.shape[0], attn.shape[2]
    step = min(32, local_rows)
    return call(
        functools.partial(add_kernel, count, width),
        (local_rows // step,),
        [
            pl.BlockSpec((1, 1, step, model), lambda i: (0, stretch, i, 0)),
            pl.BlockSpec((count, step, width), lambda i: (0, i, 0)),
        ],
        pl.BlockSpec((step, model), lambda i: (i, 0)),
        half((local_rows, model)),
        flops=2 * local_rows * model,
        moved=6 * local_rows * model,
        name="add_rows",
    )(rows, attn)


def grad_kernel(stretch, count, width, rows_ref, gain_ref, acts_ref, grad_ref, out_ref):
    rows = rows_ref[0, 0].astype(jnp.float32)
    inverse = lax.rsqrt(jnp.mean(rows * rows, axis=-1, keepdims=True) + EPSILON)
    inner = jnp.zeros_like(inverse)
    for r in range(count):
        cols = slice(r * width, (r + 1) * width)
        grad_normed = acts_ref[r].astype(jnp.float32) * gain_ref[0, stretch : stretch + 1, cols]
        inner = inner + jnp.sum(grad_normed * (rows[:, cols] * inverse), axis=-1, keepdims=True)
    mean = inner / (count * width)
    for r in range(count):
        cols = slice(r * width, (r + 1) * width)
        grad_normed = acts_ref[r].astype(jnp.float32) * gain_ref[0, stretch : stretch + 1, cols]
        grad_input = inverse * (grad_normed - rows[:, cols] * inverse * mean)
        out_ref[:, cols] = (grad_ref[0, 0, :, cols].astype(jnp.float32) + grad_input).astype(
            jnp.bfloat16
        )


def grad_rows(rows, gain, acts, grads, stretch):
    local_rows, model = rows.shape[2], rows.shape[3]
    count, width = acts.shape[0], acts.shape[2]
    step = min(32, local_rows)
    row_spec = pl.BlockSpec((1, 1, step, model), lambda i: (0, stretch, i, 0))
    return call(
        functools.partial(grad_kernel, stretch, count, width),
        (local_rows // step,),
        [
            row_spec,
            pl.BlockSpec(gain.shape, lambda i: (0, 0, 0)),
            pl.BlockSpec((count, step, width), lambda i: (0, i, 0)),
            row_spec,
        ],
        pl.BlockSpec((step, model), lambda i: (i, 0)),
        half((local_rows, model)),
        flops=10 * local_rows * model,
        moved=8 * local_rows * model,
        name="grad_rows",
    )(rows, gain, acts, grads)


def place_shifted(by, count, swap_ref, *refs):
    out_ref = refs[-1]
    swap = swap_ref[0] > 0

    @pl.when(swap)
    def _():
        for s in range(count):
            out_ref[0, (s + by) % count] = refs[s][...]

    @pl.when(jnp.logical_not(swap))
    def _():
        for s in range(count):
            out_ref[0, s] = refs[s][...]


def place_rows(arrived, swap, by):
    local_rows, model = arrived[0].shape
    count = len(arrived)
    step = min(32, local_rows)
    return call(
        functools.partial(place_shifted, by, count),
        (local_rows // step,),
        [pl.BlockSpec(memory_space=pltpu.SMEM)]
        + [pl.BlockSpec((step, model), lambda i: (i, 0))] * count,
        pl.BlockSpec((1, count, step, model), lambda i: (0, 0, i, 0)),
        half((1, count, local_rows, model)),
        moved=4 * count * local_rows * model,
        name="place_rows",
    )(swap.astype(jnp.int32).reshape(1), *arrived)


def passed_along(array, axis, by):
    count = lax.axis_size(axis)
    return lax.ppermute(array, axis, [(i, (i + by) % count) for i in range(count)])


def exchange(blocks):
    return lax.all_to_all(blocks, "ctx", split_axis=0, concat_axis=0, tiled=True)


def on_device(
    forward_in,
    backward_in,
    grad_out,
    cached_keys,
    cached_values,
    norm_gain,
    key_weight,
    value_weight,
    segment_index,
):
    count = lax.axis_size("ctx")
    stretch_count, local_rows, model = forward_in.shape[1:]
    cache_local, kv_count, head = cached_keys.shape[2:]
    tokens = local_rows * count
    width = model // count
    group_size = model // head // kv_count
    local_heads = model // head // count
    kv_local = max(1, local_heads // group_size)
    copies = max(1, group_size // local_heads)
    kv_width = kv_local * head
    assert cache_local * count <= tokens

    stretches = range(stretch_count)

    def flat(blocks):
        return blocks.reshape(tokens, width)

    def split(block):
        return block.reshape(count, local_rows, width)

    both = jnp.stack([cached_keys[0], cached_values[0]])
    both = both.reshape(2, stretch_count, cache_local, kv_count * head)
    cache_sent = jnp.stack(
        [both[..., (r // copies) * kv_width : (r // copies + 1) * kv_width] for r in range(count)]
    )

    forward, backward, grads, forward_kv, backward_kv = {}, {}, {}, {}, {}
    for s in stretches:
        forward_acts = norm_rows(forward_in, norm_gain, s, count)
        backward_acts, grad_blocks = norm_rows(backward_in, norm_gain, s, count, grad_out)
        forward[s] = flat(exchange(forward_acts))
        backward[s] = flat(exchange(backward_acts))
        grads[s] = flat(exchange(grad_blocks))
    cache = exchange(cache_sent)
    for s in stretches:
        weights = (key_weight, value_weight, s, count, kv_width, copies)
        forward_kv[s] = exchange(project(forward[s], *weights))
        backward_kv[s] = exchange(project(backward[s], *weights))
    arrived, came_back = [], []
    for s in stretches:
        attended = attention(
            segment_index, (s, 0), forward[s], forward_kv[s], cache, kv_local, head
        )
        section_out = add_rows(forward_in, exchange(split(attended)), s)
        arrived.append(passed_along(section_out, "pipe", 1))
        dq, run_sums = attention(
            segment_index, (s, 1), backward[s], backward_kv[s], cache, kv_local, head, grads[s]
        )
        every = lax.all_gather(run_sums, "ctx", axis=0, tiled=False)
        grad_acts = back_rows(dq, every, key_weight, value_weight, s, copies)
        section_grad = grad_rows(backward_in, norm_gain, exchange(split(grad_acts)), grad_out, s)
        came_back.append(passed_along(section_grad, "pipe", -1))
    rank = lax.axis_index("pipe")
    next_forward = place_rows(arrived, rank == 0, 1)
    next_backward = place_rows(came_back, rank == lax.axis_size("pipe") - 1, -1)
    return (next_forward, next_backward)


def solution(mesh):
    in_specs = (
        P("pipe", None, "ctx", None),
        P("pipe", None, "ctx", None),
        P("pipe", None, "ctx", None),
        P("pipe", None, "ctx", None, None),
        P("pipe", None, "ctx", None, None),
        P("pipe", None, None),
        P("pipe", None, "ctx", None),
        P("pipe", None, "ctx", None),
        P("pipe", None, None),
    )
    out_specs = (P("pipe", None, "ctx", None), P("pipe", None, "ctx", None))
    return jax.shard_map(
        on_device, mesh=mesh, in_specs=in_specs, out_specs=out_specs, check_vma=False
    )
```

```python
import functools

import jax
import jax.numpy as jnp
from jax import lax
from jax.experimental import pallas as pl
from jax.experimental.pallas import tpu as pltpu
from jax.sharding import PartitionSpec as P

NEGATIVE = -1e30
LOG2_E = 1.4426950408889634
EPSILON = 1e-05
VMEM_LIMIT = 50 * 1024 * 1024


def call(kernel, grid, in_specs, out_specs, out_shape, scratch=(), flops=0, moved=0, name=None):
    return pl.pallas_call(
        kernel,
        grid=grid,
        in_specs=in_specs,
        out_specs=out_specs,
        out_shape=out_shape,
        scratch_shapes=list(scratch),
        compiler_params=pltpu.CompilerParams(
            vmem_limit_bytes=VMEM_LIMIT,
            dimension_semantics=("arbitrary",) * len(grid),
        ),
        cost_estimate=pl.CostEstimate(flops=int(flops), bytes_accessed=int(moved), transcendentals=0),
        name=name,
    )


def half(shape):
    return jax.ShapeDtypeStruct(shape, jnp.bfloat16)


def nt_dot(a, b):
    return lax.dot_general(a, b, (((1,), (1,)), ((), ())), preferred_element_type=jnp.float32)


def tn_dot(a, b):
    return lax.dot_general(a, b, (((0,), (0,)), ((), ())), preferred_element_type=jnp.float32)


def nn_dot(a, b):
    return jnp.dot(a, b, preferred_element_type=jnp.float32)


def norm_kernel(stretch, count, width, has_grad, *refs):
    rows_ref, gain_ref = refs[0], refs[1]
    acts_ref = refs[-2] if has_grad else refs[-1]
    rows = rows_ref[0, 0].astype(jnp.float32)
    inverse = lax.rsqrt(jnp.mean(rows * rows, axis=-1, keepdims=True) + EPSILON)
    acts = (rows * inverse * gain_ref[0, stretch : stretch + 1, :]).astype(jnp.bfloat16)
    for r in range(count):
        acts_ref[r] = acts[:, r * width : (r + 1) * width]
        if has_grad:
            refs[-1][r] = refs[2][0, 0, :, r * width : (r + 1) * width]


def norm_rows(rows, gain, stretch, count, grad=None):
    local_rows, model = rows.shape[2], rows.shape[3]
    width = model // count
    step = min(32, local_rows)
    row_spec = pl.BlockSpec((1, 1, step, model), lambda i: (0, stretch, i, 0))
    out_spec = pl.BlockSpec((count, step, width), lambda i: (0, i, 0))
    shape = half((count, local_rows, width))
    has_grad = grad is not None
    return call(
        functools.partial(norm_kernel, stretch, count, width, has_grad),
        (local_rows // step,),
        [row_spec, pl.BlockSpec(gain.shape, lambda i: (0, 0, 0))] + [row_spec] * has_grad,
        (out_spec, out_spec) if has_grad else out_spec,
        (shape, shape) if has_grad else shape,
        flops=6 * local_rows * model,
        moved=4 * local_rows * model * (1 + has_grad),
        name="norm_rows",
    )(*((rows, gain) + ((grad,) if has_grad else ())))


def project_kernel(kv_width, rank, acts_ref, nk_ref, nv_ref, fk_ref, fv_ref, near_ref, far_ref):
    acts = acts_ref[...]
    for key_ref, value_ref, out_ref in ((nk_ref, nv_ref, near_ref), (fk_ref, fv_ref, far_ref)):
        out_ref[0, :, :kv_width] = nn_dot(acts, key_ref[0, 0]).astype(jnp.bfloat16)
        out_ref[0, :, kv_width:] = nn_dot(acts, value_ref[0, 0]).astype(jnp.bfloat16)


def project(acts, key_weight, value_weight, stretch, rank, count, kv_width, copies):
    tokens, width = acts.shape

    def weight_spec(which):
        def place(i, rank_ref):
            return (0, stretch, 0, jnp.bitwise_xor(rank_ref[0], 2 * i + which) // copies)

        return pl.BlockSpec((1, 1, width, kv_width), place)

    out_spec = pl.BlockSpec((1, tokens, 2 * kv_width), lambda i, rank_ref: (i, 0, 0))
    shape = half((count // 2, tokens, 2 * kv_width))
    return pl.pallas_call(
        functools.partial(project_kernel, kv_width),
        grid_spec=pltpu.PrefetchScalarGridSpec(
            num_scalar_prefetch=1,
            grid=(count // 2,),
            in_specs=[
                pl.BlockSpec((tokens, width), lambda i, rank_ref: (0, 0)),
                weight_spec(0),
                weight_spec(0),
                weight_spec(1),
                weight_spec(1),
            ],
            out_specs=(out_spec, out_spec),
        ),
        out_shape=(shape, shape),
        compiler_params=pltpu.CompilerParams(
            vmem_limit_bytes=VMEM_LIMIT, dimension_semantics=("arbitrary",)
        ),
        cost_estimate=pl.CostEstimate(
            flops=4 * tokens * width * kv_width * count,
            bytes_accessed=2 * (tokens * width + 2 * (width + tokens) * kv_width * count),
            transcendentals=0,
        ),
        name="project_kv",
    )(rank, acts, key_weight, value_weight, key_weight, value_weight)


def swapped(block, bit, count):
    return lax.ppermute(block, "ctx", [(i, i ^ bit) for i in range(count)])


def summed_over_ranks(near, far, count):
    bit = 1
    while True:
        arrived = swapped(far, bit, count)
        total = (near.astype(jnp.float32) + arrived.astype(jnp.float32)).astype(jnp.bfloat16)
        bit *= 2
        if bit == count:
            return total[0]
        near, far = total[0::2], total[1::2]


def load_lists(old_key, old_value, keys, values):
    keys[...] = old_key[:, 0, 0].reshape(keys.shape)
    values[...] = old_value[:, 0, 0].reshape(values.shape)


def score_pieces(queries, start, rows, cached, keys, own_keys):
    pieces = []
    if cached:
        pieces.append(nt_dot(queries, keys[...]))
    if start:
        pieces.append(nt_dot(queries, own_keys[:start]))
    diagonal = nt_dot(queries, own_keys[start : start + rows])
    column = lax.broadcasted_iota(jnp.int32, (rows, rows), 1)
    row_ids = lax.broadcasted_iota(jnp.int32, (rows, rows), 0)
    pieces.append(jnp.where(column <= row_ids, diagonal, NEGATIVE))
    return pieces


def lifted_pieces(pieces, scale):
    row_max = pieces[0].max(axis=-1, keepdims=True)
    for piece in pieces[1:]:
        row_max = jnp.maximum(row_max, piece.max(axis=-1, keepdims=True))
    lifted = [jnp.exp2((piece - row_max) * scale) for piece in pieces]
    total = lifted[0].sum(axis=-1, keepdims=True)
    for piece in lifted[1:]:
        total = total + piece.sum(axis=-1, keepdims=True)
    return lifted, 1.0 / total


def list_pieces(start, rows, cached, kept, own):
    pieces = [kept[...]] if cached else []
    if start:
        pieces.append(own[:start])
    pieces.append(own[start : start + rows])
    return pieces


def sum_of(terms):
    total = terms[0]
    for term in terms[1:]:
        total = total + term
    return total


def attend_kernel(
    head, rows, per_step, place, segment, q_ref, own_keys, own_values, ok, ov, out_ref, keys, values
):
    @pl.when(pl.program_id(1) == 0)
    def _():
        load_lists(ok, ov, keys, values)

    scale = head**-0.5 * LOG2_E
    tokens = q_ref.shape[0]

    def work(cached):
        for h in range(per_step):
            cols = slice(h * head, (h + 1) * head)
            for start in range(0, tokens, rows):
                part = slice(start, start + rows)
                queries = q_ref[part, cols]
                lifted, inverse = lifted_pieces(
                    score_pieces(queries, start, rows, cached, keys, own_keys), scale
                )
                value_pieces = list_pieces(start, rows, cached, values, own_values)
                attended = sum_of(
                    [nn_dot(e.astype(jnp.bfloat16), v) for e, v in zip(lifted, value_pieces)]
                )
                out_ref[part, cols] = (attended * inverse).astype(jnp.bfloat16)

    visible = segment[0, place[0], place[1]] > 0
    pl.when(visible)(lambda: work(True))
    pl.when(jnp.logical_not(visible))(lambda: work(False))


def attend_back_kernel(
    head, rows, per_step, place, segment, q_ref, g_ref, own_keys, own_values, ok, ov,
    dq_ref, kv_ref, keys, values, key_sum, value_sum
):
    @pl.when(pl.program_id(1) == 0)
    def _():
        load_lists(ok, ov, keys, values)
        key_sum[...] = jnp.zeros_like(key_sum)
        value_sum[...] = jnp.zeros_like(value_sum)

    factor = head**-0.5
    tokens = q_ref.shape[0]

    def work(cached):
        for h in range(per_step):
            cols = slice(h * head, (h + 1) * head)
            for start in range(0, tokens, rows):
                part = slice(start, start + rows)
                queries = q_ref[part, cols]
                grads = g_ref[part, cols]
                lifted, inverse = lifted_pieces(
                    score_pieces(queries, start, rows, cached, keys, own_keys), factor * LOG2_E
                )
                value_pieces = list_pieces(start, rows, cached, values, own_values)
                key_pieces = list_pieces(start, rows, cached, keys, own_keys)
                rounded = [e.astype(jnp.bfloat16) for e in lifted]
                attended = sum_of([nn_dot(e, v) for e, v in zip(rounded, value_pieces)]) * inverse
                wide = grads.astype(jnp.float32)
                delta = jnp.sum(wide * attended, axis=-1, keepdims=True)
                scores = [
                    (e * (nt_dot(grads, v) - delta)).astype(jnp.bfloat16)
                    for e, v in zip(lifted, value_pieces)
                ]
                row_scale = inverse * factor
                dq = sum_of([nn_dot(s, k) for s, k in zip(scores, key_pieces)]) * row_scale
                dq_ref[part, cols] = dq.astype(jnp.bfloat16)
                scaled_q = (queries.astype(jnp.float32) * row_scale).astype(jnp.bfloat16)
                scaled_g = (wide * inverse).astype(jnp.bfloat16)
                if start:
                    key_sum[:start] += tn_dot(scores[-2], scaled_q)
                    value_sum[:start] += tn_dot(rounded[-2], scaled_g)
                key_sum[part] += tn_dot(scores[-1], scaled_q)
                value_sum[part] += tn_dot(rounded[-1], scaled_g)

    visible = segment[0, place[0], place[1]] > 0
    pl.when(visible)(lambda: work(True))
    pl.when(jnp.logical_not(visible))(lambda: work(False))

    @pl.when(pl.program_id(1) == pl.num_programs(1) - 1)
    def _():
        kv_ref[0] = key_sum[...].astype(jnp.bfloat16)
        kv_ref[1] = value_sum[...].astype(jnp.bfloat16)


def attention(segment, place, queries, new_kv, cache, kv_local, head, grads=None):
    tokens, width = queries.shape
    count, cache_local = cache.shape[0], cache.shape[3]
    cache_len = count * cache_local
    sub_heads = width // head // kv_local
    per_step = 2 if sub_heads % 2 == 0 else 1
    steps = sub_heads // per_step
    rows = min(256, tokens)
    stretch = place[0]
    head_spec = pl.BlockSpec((tokens, per_step * head), lambda j, g: (0, j * steps + g))
    in_specs = [pl.BlockSpec(memory_space=pltpu.SMEM), head_spec] + [head_spec] * (grads is not None)
    in_specs += [
        pl.BlockSpec((tokens, head), lambda j, g: (0, j)),
        pl.BlockSpec((tokens, head), lambda j, g: (0, kv_local + j)),
        pl.BlockSpec((count, 1, 1, cache_local, head), lambda j, g: (0, 0, stretch, 0, j)),
        pl.BlockSpec((count, 1, 1, cache_local, head), lambda j, g: (0, 1, stretch, 0, j)),
    ]
    scratch = [pltpu.VMEM((cache_len, head), jnp.bfloat16)] * 2
    tail = (new_kv, new_kv, cache, cache)
    unit = 2 * tokens * width * (cache_len + tokens)
    if grads is None:
        return call(
            functools.partial(attend_kernel, head, rows, per_step, place),
            (kv_local, steps),
            in_specs,
            head_spec,
            half((tokens, width)),
            scratch,
            flops=2 * unit,
            moved=4 * tokens * width,
            name="attend",
        )(segment, queries, *tail)
    return call(
        functools.partial(attend_back_kernel, head, rows, per_step, place),
        (kv_local, steps),
        in_specs,
        (head_spec, pl.BlockSpec((2, tokens, head), lambda j, g: (0, 0, j))),
        (half((tokens, width)), half((2, tokens, kv_local * head))),
        scratch + [pltpu.VMEM((tokens, head), jnp.float32)] * 2,
        flops=5 * unit,
        moved=8 * tokens * width,
        name="attend_back",
    )(segment, queries, grads, *tail)


def back_kernel(count, copies, dq_ref, every_ref, key_ref, value_ref, out_ref, totals):
    kv_width = every_ref.shape[3]

    @pl.when(pl.program_id(0) == 0)
    def _():
        for which in range(2):
            for j in range(count // copies):
                total = every_ref[j * copies, which].astype(jnp.float32)
                for extra in range(1, copies):
                    total = total + every_ref[j * copies + extra, which].astype(jnp.float32)
                totals[which, :, j * kv_width : (j + 1) * kv_width] = total.astype(jnp.bfloat16)

    back = nt_dot(totals[0], key_ref[0, 0]) + nt_dot(totals[1], value_ref[0, 0])
    out_ref[...] = (dq_ref[...].astype(jnp.float32) + back).astype(jnp.bfloat16)


def back_rows(dq, every, key_weight, value_weight, stretch, copies):
    tokens, width = dq.shape
    count = every.shape[0]
    kv_total = key_weight.shape[3]
    step = min(512, width)
    weight_spec = pl.BlockSpec((1, 1, step, kv_total), lambda n: (0, stretch, n, 0))
    tile_spec = pl.BlockSpec((tokens, step), lambda n: (0, n))
    return call(
        functools.partial(back_kernel, count, copies),
        (width // step,),
        [tile_spec, pl.BlockSpec(every.shape, lambda n: (0, 0, 0, 0)), weight_spec, weight_spec],
        tile_spec,
        half((tokens, width)),
        [pltpu.VMEM((2, tokens, kv_total), jnp.bfloat16)],
        flops=4 * tokens * width * kv_total,
        moved=4 * tokens * width + 4 * width * kv_total,
        name="back_rows",
    )(dq, every, key_weight, value_weight)


def add_kernel(count, width, rows_ref, attn_ref, out_ref):
    for r in range(count):
        cols = slice(r * width, (r + 1) * width)
        out_ref[:, cols] = (
            rows_ref[0, 0, :, cols].astype(jnp.float32) + attn_ref[r].astype(jnp.float32)
        ).astype(jnp.bfloat16)


def add_rows(rows, attn, stretch):
    local_rows, model = rows.shape[2], rows.shape[3]
    count, width = attn.shape[0], attn.shape[2]
    step = min(32, local_rows)
    return call(
        functools.partial(add_kernel, count, width),
        (local_rows // step,),
        [
            pl.BlockSpec((1, 1, step, model), lambda i: (0, stretch, i, 0)),
            pl.BlockSpec((count, step, width), lambda i: (0, i, 0)),
        ],
        pl.BlockSpec((step, model), lambda i: (i, 0)),
        half((local_rows, model)),
        flops=2 * local_rows * model,
        moved=6 * local_rows * model,
        name="add_rows",
    )(rows, attn)


def grad_kernel(stretch, count, width, rows_ref, gain_ref, acts_ref, grad_ref, out_ref):
    rows = rows_ref[0, 0].astype(jnp.float32)
    inverse = lax.rsqrt(jnp.mean(rows * rows, axis=-1, keepdims=True) + EPSILON)
    inner = jnp.zeros_like(inverse)
    for r in range(count):
        cols = slice(r * width, (r + 1) * width)
        grad_normed = acts_ref[r].astype(jnp.float32) * gain_ref[0, stretch : stretch + 1, cols]
        inner = inner + jnp.sum(grad_normed * (rows[:, cols] * inverse), axis=-1, keepdims=True)
    mean = inner / (count * width)
    for r in range(count):
        cols = slice(r * width, (r + 1) * width)
        grad_normed = acts_ref[r].astype(jnp.float32) * gain_ref[0, stretch : stretch + 1, cols]
        grad_input = inverse * (grad_normed - rows[:, cols] * inverse * mean)
        out_ref[:, cols] = (grad_ref[0, 0, :, cols].astype(jnp.float32) + grad_input).astype(
            jnp.bfloat16
        )


def grad_rows(rows, gain, acts, grads, stretch):
    local_rows, model = rows.shape[2], rows.shape[3]
    count, width = acts.shape[0], acts.shape[2]
    step = min(32, local_rows)
    row_spec = pl.BlockSpec((1, 1, step, model), lambda i: (0, stretch, i, 0))
    return call(
        functools.partial(grad_kernel, stretch, count, width),
        (local_rows // step,),
        [
            row_spec,
            pl.BlockSpec(gain.shape, lambda i: (0, 0, 0)),
            pl.BlockSpec((count, step, width), lambda i: (0, i, 0)),
            row_spec,
        ],
        pl.BlockSpec((step, model), lambda i: (i, 0)),
        half((local_rows, model)),
        flops=10 * local_rows * model,
        moved=8 * local_rows * model,
        name="grad_rows",
    )(rows, gain, acts, grads)


def place_shifted(by, count, swap_ref, *refs):
    out_ref = refs[-1]
    swap = swap_ref[0] > 0

    @pl.when(swap)
    def _():
        for s in range(count):
            out_ref[0, (s + by) % count] = refs[s][...]

    @pl.when(jnp.logical_not(swap))
    def _():
        for s in range(count):
            out_ref[0, s] = refs[s][...]


def place_rows(arrived, swap, by):
    local_rows, model = arrived[0].shape
    count = len(arrived)
    step = min(32, local_rows)
    return call(
        functools.partial(place_shifted, by, count),
        (local_rows // step,),
        [pl.BlockSpec(memory_space=pltpu.SMEM)]
        + [pl.BlockSpec((step, model), lambda i: (i, 0))] * count,
        pl.BlockSpec((1, count, step, model), lambda i: (0, 0, i, 0)),
        half((1, count, local_rows, model)),
        moved=4 * count * local_rows * model,
        name="place_rows",
    )(swap.astype(jnp.int32).reshape(1), *arrived)


def passed_along(array, axis, by):
    count = lax.axis_size(axis)
    return lax.ppermute(array, axis, [(i, (i + by) % count) for i in range(count)])


def exchange(blocks):
    return lax.all_to_all(blocks, "ctx", split_axis=0, concat_axis=0, tiled=True)


def on_device(
    forward_in,
    backward_in,
    grad_out,
    cached_keys,
    cached_values,
    norm_gain,
    key_weight,
    value_weight,
    segment_index,
):
    count = lax.axis_size("ctx")
    stretch_count, local_rows, model = forward_in.shape[1:]
    cache_local, kv_count, head = cached_keys.shape[2:]
    tokens = local_rows * count
    width = model // count
    group_size = model // head // kv_count
    local_heads = model // head // count
    kv_local = max(1, local_heads // group_size)
    copies = max(1, group_size // local_heads)
    kv_width = kv_local * head
    assert cache_local * count <= tokens

    def flat(blocks):
        return blocks.reshape(tokens, width)

    def split(block):
        return block.reshape(count, local_rows, width)

    both = jnp.stack([cached_keys[0], cached_values[0]])
    both = both.reshape(2, stretch_count, cache_local, kv_count * head)
    cache_sent = jnp.stack(
        [both[..., (r // copies) * kv_width : (r // copies + 1) * kv_width] for r in range(count)]
    )

    ctx_rank = lax.axis_index("ctx").astype(jnp.int32).reshape(1)
    tie = lax.optimization_barrier
    assert stretch_count == 2

    def new_kv(acts, s):
        near, far = project(
            acts, key_weight, value_weight, s, ctx_rank, count, kv_width, copies
        )
        return near, far

    def attended(acts, kv, s):
        return attention(segment_index, (s, 0), acts, kv, cache, kv_local, head)

    def attended_back(acts, kv, s, grad):
        return attention(segment_index, (s, 1), acts, kv, cache, kv_local, head, grad)

    def gathered(run_sums):
        return lax.all_gather(run_sums, "ctx", axis=0, tiled=False)

    f0 = norm_rows(forward_in, norm_gain, 0, count)
    f0, f1, (b0, g0), cache = tie(
        (
            exchange(f0),
            norm_rows(forward_in, norm_gain, 1, count),
            norm_rows(backward_in, norm_gain, 0, count, grad_out),
            cache_sent,
        )
    )
    f0 = flat(f0)
    f1, part_f0, (b1, g1) = tie(
        (exchange(f1), new_kv(f0, 0), norm_rows(backward_in, norm_gain, 1, count, grad_out))
    )
    f1 = flat(f1)
    kv_f0 = summed_over_ranks(*part_f0, count)
    cache, part_f1, kv_f0, b0 = tie((exchange(cache), new_kv(f1, 1), kv_f0, b0))
    kv_f1 = summed_over_ranks(*part_f1, count)
    b0, a0, kv_f1, cache = tie((exchange(b0), attended(f0, kv_f0, 0), kv_f1, cache))
    b0 = flat(b0)
    a0, part_b0, a1, g0 = tie((exchange(split(a0)), new_kv(b0, 0), attended(f1, kv_f1, 1), g0))
    kv_b0 = summed_over_ranks(*part_b0, count)
    g0, o0, kv_b0, b1 = tie((exchange(g0), add_rows(forward_in, a0, 0), kv_b0, b1))
    arrived0 = passed_along(o0, "pipe", 1)
    b1, (dq0, runs0), g1 = tie((exchange(b1), attended_back(b0, kv_b0, 0, flat(g0)), g1))
    b1 = flat(b1)
    every0 = gathered(runs0)
    part_b1 = new_kv(b1, 1)
    kv_b1 = summed_over_ranks(*part_b1, count)
    ga0 = back_rows(dq0, every0, key_weight, value_weight, 0, copies)
    g1, kv_b1, ga0, a1, arrived0 = tie((exchange(g1), kv_b1, ga0, a1, arrived0))
    a1, (dq1, runs1), ga0 = tie(
        (exchange(split(a1)), attended_back(b1, kv_b1, 1, flat(g1)), ga0)
    )
    every1 = gathered(runs1)
    o1 = add_rows(forward_in, a1, 1)
    ga1 = back_rows(dq1, every1, key_weight, value_weight, 1, copies)
    ga0, ga1, o1 = tie((exchange(split(ga0)), ga1, o1))
    r0 = grad_rows(backward_in, norm_gain, ga0, grad_out, 0)
    r0, arrived1 = tie((r0, passed_along(o1, "pipe", 1)))
    came0 = passed_along(r0, "pipe", -1)
    r1 = grad_rows(backward_in, norm_gain, exchange(split(ga1)), grad_out, 1)
    came1 = passed_along(r1, "pipe", -1)
    arrived, came_back = [arrived0, arrived1], [came0, came1]
    rank = lax.axis_index("pipe")
    next_forward = place_rows(arrived, rank == 0, 1)
    next_backward = place_rows(came_back, rank == lax.axis_size("pipe") - 1, -1)
    return (next_forward, next_backward)


def solution(mesh):
    in_specs = (
        P("pipe", None, "ctx", None),
        P("pipe", None, "ctx", None),
        P("pipe", None, "ctx", None),
        P("pipe", None, "ctx", None, None),
        P("pipe", None, "ctx", None, None),
        P("pipe", None, None),
        P("pipe", None, "ctx", None),
        P("pipe", None, "ctx", None),
        P("pipe", None, None),
    )
    out_specs = (P("pipe", None, "ctx", None), P("pipe", None, "ctx", None))
    return jax.shard_map(
        on_device, mesh=mesh, in_specs=in_specs, out_specs=out_specs, check_vma=False
    )
```

```python
import functools

import jax
import jax.numpy as jnp
from jax import lax
from jax.experimental import pallas as pl
from jax.experimental.pallas import tpu as pltpu
from jax.sharding import PartitionSpec as P

NEGATIVE = -1e30
LOG2_E = 1.4426950408889634
EPSILON = 1e-05
VMEM_LIMIT = 50 * 1024 * 1024


def call(kernel, grid, in_specs, out_specs, out_shape, scratch=(), flops=0, moved=0, name=None):
    return pl.pallas_call(
        kernel,
        grid=grid,
        in_specs=in_specs,
        out_specs=out_specs,
        out_shape=out_shape,
        scratch_shapes=list(scratch),
        compiler_params=pltpu.CompilerParams(
            vmem_limit_bytes=VMEM_LIMIT,
            dimension_semantics=("arbitrary",) * len(grid),
        ),
        cost_estimate=pl.CostEstimate(flops=int(flops), bytes_accessed=int(moved), transcendentals=0),
        name=name,
    )


def half(shape):
    return jax.ShapeDtypeStruct(shape, jnp.bfloat16)


def nt_dot(a, b):
    return lax.dot_general(a, b, (((1,), (1,)), ((), ())), preferred_element_type=jnp.float32)


def tn_dot(a, b):
    return lax.dot_general(a, b, (((0,), (0,)), ((), ())), preferred_element_type=jnp.float32)


def nn_dot(a, b):
    return jnp.dot(a, b, preferred_element_type=jnp.float32)


def norm_kernel(stretch, count, width, has_grad, *refs):
    rows_ref, gain_ref = refs[0], refs[1]
    acts_ref = refs[-2] if has_grad else refs[-1]
    rows = rows_ref[0, 0].astype(jnp.float32)
    inverse = lax.rsqrt(jnp.mean(rows * rows, axis=-1, keepdims=True) + EPSILON)
    acts = (rows * inverse * gain_ref[0, stretch : stretch + 1, :]).astype(jnp.bfloat16)
    for r in range(count):
        acts_ref[r] = acts[:, r * width : (r + 1) * width]
        if has_grad:
            refs[-1][r] = refs[2][0, 0, :, r * width : (r + 1) * width]


def norm_rows(rows, gain, stretch, count, grad=None):
    local_rows, model = rows.shape[2], rows.shape[3]
    width = model // count
    step = min(32, local_rows)
    row_spec = pl.BlockSpec((1, 1, step, model), lambda i: (0, stretch, i, 0))
    out_spec = pl.BlockSpec((count, step, width), lambda i: (0, i, 0))
    shape = half((count, local_rows, width))
    has_grad = grad is not None
    return call(
        functools.partial(norm_kernel, stretch, count, width, has_grad),
        (local_rows // step,),
        [row_spec, pl.BlockSpec(gain.shape, lambda i: (0, 0, 0))] + [row_spec] * has_grad,
        (out_spec, out_spec) if has_grad else out_spec,
        (shape, shape) if has_grad else shape,
        flops=6 * local_rows * model,
        moved=4 * local_rows * model * (1 + has_grad),
        name="norm_rows",
    )(*((rows, gain) + ((grad,) if has_grad else ())))


def project_kernel(kv_width, rank, acts_ref, nk_ref, nv_ref, fk_ref, fv_ref, near_ref, far_ref):
    acts = acts_ref[...]
    for key_ref, value_ref, out_ref in ((nk_ref, nv_ref, near_ref), (fk_ref, fv_ref, far_ref)):
        out_ref[0, :, :kv_width] = nn_dot(acts, key_ref[0, 0]).astype(jnp.bfloat16)
        out_ref[0, :, kv_width:] = nn_dot(acts, value_ref[0, 0]).astype(jnp.bfloat16)


def project(acts, key_weight, value_weight, stretch, rank, count, kv_width, copies):
    tokens, width = acts.shape

    def weight_spec(which):
        def place(i, rank_ref):
            return (0, stretch, 0, jnp.bitwise_xor(rank_ref[0], 2 * i + which) // copies)

        return pl.BlockSpec((1, 1, width, kv_width), place)

    out_spec = pl.BlockSpec((1, tokens, 2 * kv_width), lambda i, rank_ref: (i, 0, 0))
    shape = half((count // 2, tokens, 2 * kv_width))
    return pl.pallas_call(
        functools.partial(project_kernel, kv_width),
        grid_spec=pltpu.PrefetchScalarGridSpec(
            num_scalar_prefetch=1,
            grid=(count // 2,),
            in_specs=[
                pl.BlockSpec((tokens, width), lambda i, rank_ref: (0, 0)),
                weight_spec(0),
                weight_spec(0),
                weight_spec(1),
                weight_spec(1),
            ],
            out_specs=(out_spec, out_spec),
        ),
        out_shape=(shape, shape),
        compiler_params=pltpu.CompilerParams(
            vmem_limit_bytes=VMEM_LIMIT, dimension_semantics=("arbitrary",)
        ),
        cost_estimate=pl.CostEstimate(
            flops=4 * tokens * width * kv_width * count,
            bytes_accessed=2 * (tokens * width + 2 * (width + tokens) * kv_width * count),
            transcendentals=0,
        ),
        name="project_kv",
    )(rank, acts, key_weight, value_weight, key_weight, value_weight)


def swapped(block, bit, count):
    return lax.ppermute(block, "ctx", [(i, i ^ bit) for i in range(count)])


def summed_over_ranks(near, far, count):
    bit = 1
    while True:
        arrived = swapped(far, bit, count)
        total = (near.astype(jnp.float32) + arrived.astype(jnp.float32)).astype(jnp.bfloat16)
        bit *= 2
        if bit == count:
            return total[0]
        near, far = total[0::2], total[1::2]


def load_lists(old_key, old_value, keys, values):
    keys[...] = old_key[:, 0, 0].reshape(keys.shape)
    values[...] = old_value[:, 0, 0].reshape(values.shape)


def score_pieces(queries, start, rows, cached, keys, own_keys):
    pieces = []
    if cached:
        pieces.append(nt_dot(queries, keys[...]))
    if start:
        pieces.append(nt_dot(queries, own_keys[:start]))
    diagonal = nt_dot(queries, own_keys[start : start + rows])
    column = lax.broadcasted_iota(jnp.int32, (rows, rows), 1)
    row_ids = lax.broadcasted_iota(jnp.int32, (rows, rows), 0)
    pieces.append(jnp.where(column <= row_ids, diagonal, NEGATIVE))
    return pieces


def lifted_pieces(pieces, scale):
    row_max = pieces[0].max(axis=-1, keepdims=True)
    for piece in pieces[1:]:
        row_max = jnp.maximum(row_max, piece.max(axis=-1, keepdims=True))
    lifted = [jnp.exp2((piece - row_max) * scale) for piece in pieces]
    total = lifted[0].sum(axis=-1, keepdims=True)
    for piece in lifted[1:]:
        total = total + piece.sum(axis=-1, keepdims=True)
    return lifted, 1.0 / total


def list_pieces(start, rows, cached, kept, own):
    pieces = [kept[...]] if cached else []
    if start:
        pieces.append(own[:start])
    pieces.append(own[start : start + rows])
    return pieces


def sum_of(terms):
    total = terms[0]
    for term in terms[1:]:
        total = total + term
    return total


def attend_kernel(
    head, rows, per_step, place, segment, q_ref, own_keys, own_values, ok, ov, out_ref, keys, values
):
    @pl.when(pl.program_id(1) == 0)
    def _():
        load_lists(ok, ov, keys, values)

    scale = head**-0.5 * LOG2_E
    tokens = q_ref.shape[0]

    def work(cached):
        for h in range(per_step):
            cols = slice(h * head, (h + 1) * head)
            for start in range(0, tokens, rows):
                part = slice(start, start + rows)
                queries = q_ref[part, cols]
                lifted, inverse = lifted_pieces(
                    score_pieces(queries, start, rows, cached, keys, own_keys), scale
                )
                value_pieces = list_pieces(start, rows, cached, values, own_values)
                attended = sum_of(
                    [nn_dot(e.astype(jnp.bfloat16), v) for e, v in zip(lifted, value_pieces)]
                )
                out_ref[part, cols] = (attended * inverse).astype(jnp.bfloat16)

    visible = segment[0, place[0], place[1]] > 0
    pl.when(visible)(lambda: work(True))
    pl.when(jnp.logical_not(visible))(lambda: work(False))


def attend_back_kernel(
    head, rows, per_step, place, segment, q_ref, g_ref, own_keys, own_values, ok, ov,
    dq_ref, kv_ref, keys, values, key_sum, value_sum
):
    @pl.when(pl.program_id(1) == 0)
    def _():
        load_lists(ok, ov, keys, values)
        key_sum[...] = jnp.zeros_like(key_sum)
        value_sum[...] = jnp.zeros_like(value_sum)

    factor = head**-0.5
    tokens = q_ref.shape[0]

    def work(cached):
        for h in range(per_step):
            cols = slice(h * head, (h + 1) * head)
            for start in range(0, tokens, rows):
                part = slice(start, start + rows)
                queries = q_ref[part, cols]
                grads = g_ref[part, cols]
                lifted, inverse = lifted_pieces(
                    score_pieces(queries, start, rows, cached, keys, own_keys), factor * LOG2_E
                )
                value_pieces = list_pieces(start, rows, cached, values, own_values)
                key_pieces = list_pieces(start, rows, cached, keys, own_keys)
                rounded = [e.astype(jnp.bfloat16) for e in lifted]
                attended = sum_of([nn_dot(e, v) for e, v in zip(rounded, value_pieces)]) * inverse
                wide = grads.astype(jnp.float32)
                delta = jnp.sum(wide * attended, axis=-1, keepdims=True)
                scores = [
                    (e * (nt_dot(grads, v) - delta)).astype(jnp.bfloat16)
                    for e, v in zip(lifted, value_pieces)
                ]
                row_scale = inverse * factor
                dq = sum_of([nn_dot(s, k) for s, k in zip(scores, key_pieces)]) * row_scale
                dq_ref[part, cols] = dq.astype(jnp.bfloat16)
                scaled_q = (queries.astype(jnp.float32) * row_scale).astype(jnp.bfloat16)
                scaled_g = (wide * inverse).astype(jnp.bfloat16)
                if start:
                    key_sum[:start] += tn_dot(scores[-2], scaled_q)
                    value_sum[:start] += tn_dot(rounded[-2], scaled_g)
                key_sum[part] += tn_dot(scores[-1], scaled_q)
                value_sum[part] += tn_dot(rounded[-1], scaled_g)

    visible = segment[0, place[0], place[1]] > 0
    pl.when(visible)(lambda: work(True))
    pl.when(jnp.logical_not(visible))(lambda: work(False))

    @pl.when(pl.program_id(1) == pl.num_programs(1) - 1)
    def _():
        kv_ref[0] = key_sum[...].astype(jnp.bfloat16)
        kv_ref[1] = value_sum[...].astype(jnp.bfloat16)


def attention(segment, place, queries, new_kv, cache, kv_local, head, grads=None):
    tokens, width = queries.shape
    count, cache_local = cache.shape[0], cache.shape[3]
    cache_len = count * cache_local
    sub_heads = width // head // kv_local
    per_step = 2 if sub_heads % 2 == 0 else 1
    steps = sub_heads // per_step
    rows = min(256, tokens)
    stretch = place[0]
    head_spec = pl.BlockSpec((tokens, per_step * head), lambda j, g: (0, j * steps + g))
    in_specs = [pl.BlockSpec(memory_space=pltpu.SMEM), head_spec] + [head_spec] * (grads is not None)
    in_specs += [
        pl.BlockSpec((tokens, head), lambda j, g: (0, j)),
        pl.BlockSpec((tokens, head), lambda j, g: (0, kv_local + j)),
        pl.BlockSpec((count, 1, 1, cache_local, head), lambda j, g: (0, 0, stretch, 0, j)),
        pl.BlockSpec((count, 1, 1, cache_local, head), lambda j, g: (0, 1, stretch, 0, j)),
    ]
    scratch = [pltpu.VMEM((cache_len, head), jnp.bfloat16)] * 2
    tail = (new_kv, new_kv, cache, cache)
    unit = 2 * tokens * width * (cache_len + tokens)
    if grads is None:
        return call(
            functools.partial(attend_kernel, head, rows, per_step, place),
            (kv_local, steps),
            in_specs,
            head_spec,
            half((tokens, width)),
            scratch,
            flops=2 * unit,
            moved=4 * tokens * width,
            name="attend",
        )(segment, queries, *tail)
    return call(
        functools.partial(attend_back_kernel, head, rows, per_step, place),
        (kv_local, steps),
        in_specs,
        (head_spec, pl.BlockSpec((2, tokens, head), lambda j, g: (0, 0, j))),
        (half((tokens, width)), half((2, tokens, kv_local * head))),
        scratch + [pltpu.VMEM((tokens, head), jnp.float32)] * 2,
        flops=5 * unit,
        moved=8 * tokens * width,
        name="attend_back",
    )(segment, queries, grads, *tail)


def back_kernel(count, copies, dq_ref, every_ref, key_ref, value_ref, out_ref, totals):
    kv_width = every_ref.shape[3]

    @pl.when(pl.program_id(0) == 0)
    def _():
        for which in range(2):
            for j in range(count // copies):
                total = every_ref[j * copies, which].astype(jnp.float32)
                for extra in range(1, copies):
                    total = total + every_ref[j * copies + extra, which].astype(jnp.float32)
                totals[which, :, j * kv_width : (j + 1) * kv_width] = total.astype(jnp.bfloat16)

    back = nt_dot(totals[0], key_ref[0, 0]) + nt_dot(totals[1], value_ref[0, 0])
    out_ref[...] = (dq_ref[...].astype(jnp.float32) + back).astype(jnp.bfloat16)


def back_rows(dq, every, key_weight, value_weight, stretch, copies):
    tokens, width = dq.shape
    count = every.shape[0]
    kv_total = key_weight.shape[3]
    step = min(512, width)
    weight_spec = pl.BlockSpec((1, 1, step, kv_total), lambda n: (0, stretch, n, 0))
    tile_spec = pl.BlockSpec((tokens, step), lambda n: (0, n))
    return call(
        functools.partial(back_kernel, count, copies),
        (width // step,),
        [tile_spec, pl.BlockSpec(every.shape, lambda n: (0, 0, 0, 0)), weight_spec, weight_spec],
        tile_spec,
        half((tokens, width)),
        [pltpu.VMEM((2, tokens, kv_total), jnp.bfloat16)],
        flops=4 * tokens * width * kv_total,
        moved=4 * tokens * width + 4 * width * kv_total,
        name="back_rows",
    )(dq, every, key_weight, value_weight)


def add_kernel(count, width, rows_ref, attn_ref, out_ref):
    for r in range(count):
        cols = slice(r * width, (r + 1) * width)
        out_ref[:, cols] = (
            rows_ref[0, 0, :, cols].astype(jnp.float32) + attn_ref[r].astype(jnp.float32)
        ).astype(jnp.bfloat16)


def add_rows(rows, attn, stretch):
    local_rows, model = rows.shape[2], rows.shape[3]
    count, width = attn.shape[0], attn.shape[2]
    step = min(32, local_rows)
    return call(
        functools.partial(add_kernel, count, width),
        (local_rows // step,),
        [
            pl.BlockSpec((1, 1, step, model), lambda i: (0, stretch, i, 0)),
            pl.BlockSpec((count, step, width), lambda i: (0, i, 0)),
        ],
        pl.BlockSpec((step, model), lambda i: (i, 0)),
        half((local_rows, model)),
        flops=2 * local_rows * model,
        moved=6 * local_rows * model,
        name="add_rows",
    )(rows, attn)


def grad_kernel(stretch, count, width, rows_ref, gain_ref, acts_ref, grad_ref, out_ref):
    rows = rows_ref[0, 0].astype(jnp.float32)
    inverse = lax.rsqrt(jnp.mean(rows * rows, axis=-1, keepdims=True) + EPSILON)
    inner = jnp.zeros_like(inverse)
    for r in range(count):
        cols = slice(r * width, (r + 1) * width)
        grad_normed = acts_ref[r].astype(jnp.float32) * gain_ref[0, stretch : stretch + 1, cols]
        inner = inner + jnp.sum(grad_normed * (rows[:, cols] * inverse), axis=-1, keepdims=True)
    mean = inner / (count * width)
    for r in range(count):
        cols = slice(r * width, (r + 1) * width)
        grad_normed = acts_ref[r].astype(jnp.float32) * gain_ref[0, stretch : stretch + 1, cols]
        grad_input = inverse * (grad_normed - rows[:, cols] * inverse * mean)
        out_ref[:, cols] = (grad_ref[0, 0, :, cols].astype(jnp.float32) + grad_input).astype(
            jnp.bfloat16
        )


def grad_rows(rows, gain, acts, grads, stretch):
    local_rows, model = rows.shape[2], rows.shape[3]
    count, width = acts.shape[0], acts.shape[2]
    step = min(32, local_rows)
    row_spec = pl.BlockSpec((1, 1, step, model), lambda i: (0, stretch, i, 0))
    return call(
        functools.partial(grad_kernel, stretch, count, width),
        (local_rows // step,),
        [
            row_spec,
            pl.BlockSpec(gain.shape, lambda i: (0, 0, 0)),
            pl.BlockSpec((count, step, width), lambda i: (0, i, 0)),
            row_spec,
        ],
        pl.BlockSpec((step, model), lambda i: (i, 0)),
        half((local_rows, model)),
        flops=10 * local_rows * model,
        moved=8 * local_rows * model,
        name="grad_rows",
    )(rows, gain, acts, grads)


def place_shifted(by, count, swap_ref, *refs):
    out_ref = refs[-1]
    swap = swap_ref[0] > 0

    @pl.when(swap)
    def _():
        for s in range(count):
            out_ref[0, (s + by) % count] = refs[s][...]

    @pl.when(jnp.logical_not(swap))
    def _():
        for s in range(count):
            out_ref[0, s] = refs[s][...]


def place_rows(arrived, swap, by):
    local_rows, model = arrived[0].shape
    count = len(arrived)
    step = min(32, local_rows)
    return call(
        functools.partial(place_shifted, by, count),
        (local_rows // step,),
        [pl.BlockSpec(memory_space=pltpu.SMEM)]
        + [pl.BlockSpec((step, model), lambda i: (i, 0))] * count,
        pl.BlockSpec((1, count, step, model), lambda i: (0, 0, i, 0)),
        half((1, count, local_rows, model)),
        moved=4 * count * local_rows * model,
        name="place_rows",
    )(swap.astype(jnp.int32).reshape(1), *arrived)


def passed_along(array, axis, by):
    count = lax.axis_size(axis)
    return lax.ppermute(array, axis, [(i, (i + by) % count) for i in range(count)])


def exchange(blocks):
    return lax.all_to_all(blocks, "ctx", split_axis=0, concat_axis=0, tiled=True)


def on_device(
    forward_in,
    backward_in,
    grad_out,
    cached_keys,
    cached_values,
    norm_gain,
    key_weight,
    value_weight,
    segment_index,
):
    count = lax.axis_size("ctx")
    stretch_count, local_rows, model = forward_in.shape[1:]
    cache_local, kv_count, head = cached_keys.shape[2:]
    tokens = local_rows * count
    width = model // count
    group_size = model // head // kv_count
    local_heads = model // head // count
    kv_local = max(1, local_heads // group_size)
    copies = max(1, group_size // local_heads)
    kv_width = kv_local * head
    assert cache_local * count <= tokens

    def flat(blocks):
        return blocks.reshape(tokens, width)

    def split(block):
        return block.reshape(count, local_rows, width)

    both = jnp.stack([cached_keys[0], cached_values[0]])
    both = both.reshape(2, stretch_count, cache_local, kv_count * head)
    cache_sent = jnp.stack(
        [both[..., (r // copies) * kv_width : (r // copies + 1) * kv_width] for r in range(count)]
    )

    ctx_rank = lax.axis_index("ctx").astype(jnp.int32).reshape(1)
    tie = lax.optimization_barrier
    assert stretch_count == 2

    def new_kv(acts, s):
        near, far = project(
            acts, key_weight, value_weight, s, ctx_rank, count, kv_width, copies
        )
        return near, far

    def attended(acts, kv, s):
        return attention(segment_index, (s, 0), acts, kv, cache, kv_local, head)

    def attended_back(acts, kv, s, grad):
        return attention(segment_index, (s, 1), acts, kv, cache, kv_local, head, grad)

    def gathered(run_sums):
        return lax.all_gather(run_sums, "ctx", axis=0, tiled=False)

    f0 = norm_rows(forward_in, norm_gain, 0, count)
    f0, f1, (b0, g0), cache = tie(
        (
            exchange(f0),
            norm_rows(forward_in, norm_gain, 1, count),
            norm_rows(backward_in, norm_gain, 0, count, grad_out),
            cache_sent,
        )
    )
    f0 = flat(f0)
    f1, part_f0, (b1, g1) = tie(
        (exchange(f1), new_kv(f0, 0), norm_rows(backward_in, norm_gain, 1, count, grad_out))
    )
    f1 = flat(f1)
    kv_f0 = summed_over_ranks(*part_f0, count)
    cache, part_f1, kv_f0, b0 = tie((exchange(cache), new_kv(f1, 1), kv_f0, b0))
    kv_f1 = summed_over_ranks(*part_f1, count)
    b0, a0, kv_f1, cache = tie((exchange(b0), attended(f0, kv_f0, 0), kv_f1, cache))
    b0 = flat(b0)
    a0, part_b0, a1, g0 = tie((exchange(split(a0)), new_kv(b0, 0), attended(f1, kv_f1, 1), g0))
    kv_b0 = summed_over_ranks(*part_b0, count)
    g0, o0, kv_b0, b1 = tie((exchange(g0), add_rows(forward_in, a0, 0), kv_b0, b1))
    arrived0 = passed_along(o0, "pipe", 1)
    b1, (dq0, runs0), g1 = tie((exchange(b1), attended_back(b0, kv_b0, 0, flat(g0)), g1))
    b1 = flat(b1)
    every0 = gathered(runs0)
    part_b1 = new_kv(b1, 1)
    kv_b1 = summed_over_ranks(*part_b1, count)
    ga0 = back_rows(dq0, every0, key_weight, value_weight, 0, copies)
    g1, kv_b1, ga0, a1, arrived0 = tie((exchange(g1), kv_b1, ga0, a1, arrived0))
    a1, (dq1, runs1), ga0 = tie(
        (exchange(split(a1)), attended_back(b1, kv_b1, 1, flat(g1)), ga0)
    )
    every1 = gathered(runs1)
    o1 = add_rows(forward_in, a1, 1)
    ga1 = back_rows(dq1, every1, key_weight, value_weight, 1, copies)
    ga0, ga1, o1 = tie((exchange(split(ga0)), ga1, o1))
    r0 = grad_rows(backward_in, norm_gain, ga0, grad_out, 0)
    arrived1 = passed_along(o1, "pipe", 1)
    came0 = passed_along(r0, "pipe", -1)
    r1 = grad_rows(backward_in, norm_gain, exchange(split(ga1)), grad_out, 1)
    came1 = passed_along(r1, "pipe", -1)
    arrived, came_back = [arrived0, arrived1], [came0, came1]
    rank = lax.axis_index("pipe")
    next_forward = place_rows(arrived, rank == 0, 1)
    next_backward = place_rows(came_back, rank == lax.axis_size("pipe") - 1, -1)
    return (next_forward, next_backward)


def solution(mesh):
    in_specs = (
        P("pipe", None, "ctx", None),
        P("pipe", None, "ctx", None),
        P("pipe", None, "ctx", None),
        P("pipe", None, "ctx", None, None),
        P("pipe", None, "ctx", None, None),
        P("pipe", None, None),
        P("pipe", None, "ctx", None),
        P("pipe", None, "ctx", None),
        P("pipe", None, None),
    )
    out_specs = (P("pipe", None, "ctx", None), P("pipe", None, "ctx", None))
    return jax.shard_map(
        on_device, mesh=mesh, in_specs=in_specs, out_specs=out_specs, check_vma=False
    )
```
